256 devices in a mesh: frame: 8 (over x_lo, y), head: 16 (over z, x_hi), rep: 2 (over core).
Axes of the slice: x: 4 (x_hi: 2, x_lo: 2; x = x_hi * 2 + x_lo), y: 4, z: 8, core: 2. Of those that a mesh axis runs over, the one named last changes fastest.
Arguments:
- queries: bfloat16 [16, 4096, 2048], P(('rep', 'frame'), 'head'), parts along dimension 0, may hold values from -80 to 80
- keys: bfloat16 [16, 4096, 2048], P(('rep', 'frame'), 'head'), parts along dimension 0, may hold values from -4.1 to 4.1
- values: bfloat16 [16, 4096, 2048], P(('rep', 'frame'), 'head'), parts along dimension 0, may hold values from -6 to 6
- head_class: int32 [16], replicated, may hold values from 0 to 1, as said below
- w_out: bfloat16 [2048, 3072], P('head'), may hold values from -0.125 to 0.125
Outputs:
- mixed: bfloat16 [16, 4096, 3072], P(('rep', 'frame'), 'head'), parts along dimension 0
The draws below stay inside these ranges and needn't reach their ends.
There are 2 independent parts, one for each index of `rep`. The reference program is written for one: setup_inputs(seed, part) draws one part's arguments, and reference() takes and returns one part's arrays. A program takes and returns all parts, laid end to end along the dimension named above; an argument that names none is the same for every part. Nothing has to cross between parts.
Inputs may be any that keep to these rules, and one draw needn't show every extreme that they name: `head_class`: both classes occur among the heads.
All inputs are finite; a program needn't handle non-finite values.
Results may differ from the reference program's by a relative error of at most 0.012.
Values may be sent and summed in bfloat16 or wider, within the bound.
A program may use at most 128 MiB of HBM per device.

```python
import jax
import jax.numpy as jnp
from jax import lax

D = 3072
HEAD_SIZE = 128
HEADS = 16
PATCHES = 4096
FRAMES = 8


def key_base(key):
    return jnp.clip(jax.random.normal(key, (FRAMES, PATCHES, HEADS * HEAD_SIZE), jnp.float32), -4.0, 4.0)


def draw_queries(key, part):
    key = jax.random.fold_in(key, 11)
    drawn = jnp.clip(jax.random.normal(key, (FRAMES, PATCHES, HEADS * HEAD_SIZE), jnp.float32), -4.0, 4.0)
    return drawn.astype(jnp.bfloat16)


def draw_keys(key, part):
    base = key_base(key)
    attended_output = base
    return attended_output.astype(jnp.bfloat16)


def draw_head_class(key, part):
    key = jax.random.fold_in(key, 7)
    first_key, second_key = jax.random.split(key)
    kinds = jax.random.randint(first_key, (HEADS,), 0, 2).astype(jnp.int32)
    order = jax.random.permutation(second_key, HEADS)
    kinds = kinds.at[order[0]].set(0)
    kinds = kinds.at[order[1]].set(1)
    return kinds


def steps_of(own_key, shape, cuts, least, top_value):
    factor_of = 1.0
    for axis_at, blocks in cuts:
        heights = jax.random.uniform(jax.random.fold_in(jax.random.fold_in(own_key, 6), axis_at), (blocks,), jnp.float32, least / len(cuts), top_value / len(cuts))
        factor_of = factor_of * jnp.repeat(jnp.exp(heights), shape[axis_at] // blocks).reshape((-1,) + (1,) * (len(shape) - 1 - axis_at))
    return factor_of


def scatter_about(stream_key, shape, deviation, limit, pieces=(), dtype=jnp.bfloat16):
    values = jax.random.normal(stream_key, shape, jnp.float32) * deviation
    if len(pieces) > 0:
        values = steps_of(stream_key, shape, pieces, -0.22, 0.18) * values
    return jnp.clip(values, min=-limit, max=limit).astype(dtype)


def setup_inputs(seed: int = 0, part: int = 0) -> dict:
    arg_keys = jax.random.split(jax.random.key(seed), 6)
    own_keys = jax.random.split(jax.random.fold_in(arg_keys[5], part), 6)
    return {
        "queries": draw_queries(jax.random.fold_in(jax.random.fold_in(arg_keys[5], part), 71), part),
        "keys": draw_keys(jax.random.fold_in(jax.random.fold_in(arg_keys[5], part), 71), part),
        "values": scatter_about(own_keys[2], (FRAMES, PATCHES, HEADS * HEAD_SIZE), 1.0, 6.0, ((0, 8), (1, 16))),
        "head_class": draw_head_class(jax.random.fold_in(arg_keys[5], 71), part),
        "w_out": scatter_about(arg_keys[4], (HEADS * HEAD_SIZE, D), (HEADS * HEAD_SIZE) ** -0.5, 0.125, ((0, 16),)),
    }


def attend(query_group, key_group, value_group):
    logit_scores = jnp.einsum("zhd,znd->zhn", query_group.astype(jnp.float32), key_group.astype(jnp.float32)) * (HEAD_SIZE ** -0.5)
    row_max = jnp.max(logit_scores, axis=-1, keepdims=True)
    expos = jnp.exp(logit_scores - row_max)
    row_total_sum = jnp.sum(expos, axis=-1, keepdims=True)
    softmax_weights = expos.astype(jnp.bfloat16)
    attended_output = jnp.einsum("smv,svd->smd", softmax_weights.astype(jnp.float32), value_group.astype(jnp.float32)) / row_total_sum
    return attended_output.astype(jnp.bfloat16)


def one_head(operands):
    query_head, key_head, value_head, head_kind = operands

    def spatial():
        return lax.map(lambda frame_set: attend(frame_set[0][None], frame_set[1][None], frame_set[2][None])[0], (query_head, key_head, value_head))

    def temporal():
        attended_output = attend(query_head.transpose(1, 0, 2), key_head.transpose(1, 0, 2), value_head.transpose(1, 0, 2))
        return attended_output.transpose(1, 0, 2)

    return lax.cond(head_kind == 0, spatial, temporal)


def reference(queries, keys, values, head_class, w_out):
    def split_heads(array):
        return array.reshape(FRAMES, PATCHES, HEADS, HEAD_SIZE).transpose(2, 0, 1, 3)

    heads_out = lax.map(one_head, (split_heads(queries), split_heads(keys), split_heads(values), head_class))
    attn = heads_out.transpose(1, 2, 0, 3).reshape(FRAMES * PATCHES, HEADS * HEAD_SIZE)
    mixed = jnp.dot(attn, w_out, preferred_element_type=jnp.float32).astype(jnp.bfloat16)
    return mixed.reshape(FRAMES, PATCHES, D)
```

```python
import functools

import jax
import jax.numpy as jnp
from jax import lax
from jax.experimental import pallas as pl
from jax.experimental.pallas import tpu as pltpu
from jax.sharding import PartitionSpec as P

HEADS = 16
HEAD = 128
ROWS = 256
PART = 32
FRAMES = 8
WIDE = 3072
HALF = WIDE // 2
QUARTER = WIDE // 4
DEEP = 64
SCALE = HEAD**-0.5 * 1.4426950408889634
MESH = pl.DeviceIdType.MESH

PLANS = (6, 8, 10, 15)


def dot_nt(a, b):
    return lax.dot_general(a, b, (((1,), (1,)), ((), ())), preferred_element_type=jnp.float32)


def around(i):
    return 8 + lax.div(i + 1, 2) * (2 * lax.rem(i, 2) - 1)


def hosts_of(count):
    return [(k * 8) // count for k in range(count)]


def hosted(spatial, level, zz):
    count = min(spatial, 8) if level == 0 else spatial - 8
    if count == 8:
        return None, zz + 8 * level
    hosts = hosts_of(count)
    there = sum((zz == k).astype(jnp.int32) for k in hosts)
    slot = sum((zz > k).astype(jnp.int32) for k in hosts)
    return there == 1, slot + 8 * level


def only(condition, body):
    if condition is None:
        body()
    else:
        pl.when(condition)(body)


def kernel(
    spatial, temporal, hc, q_in, k_in, v_in, w_in, out,
    raw, st, kv, qb, tb, ot, ost, at, cat, wf, sbuf, acc,
    s_kv, r_kv, s_q, r_q, s_x, r_x, s_o, r_o, s_t, r_t, s_to, r_to,
    s_wz, r_wz, s_wc, r_wc, s_wy, r_wy, s_wd, r_wd,
):
    levels = 1 if spatial <= 8 else 2
    first_t = HEADS - temporal
    f, h, c = lax.axis_index("frame"), lax.axis_index("head"), lax.axis_index("rep")
    xl, y = lax.div(f, 4), lax.rem(f, 4)
    z, xh = lax.div(h, 2), lax.rem(h, 2)
    par = lax.rem(y, 2)

    def at_z(zz):
        return (f, lax.rem(zz, 8) * 2 + xh, c)

    def at_frame(ff):
        return (ff, h, c)

    def at_y(step):
        return (xl * 4 + lax.rem(y + step + 4, 4), h, c)

    partner = (f, z * 2 + 1 - xh, c)
    cross = ((1 - xl) * 4 + y, z * 2 + 1 - xh, c)
    twin = (f, h, 1 - c)

    def copy(src, dst, send, recv, to):
        return pltpu.make_async_remote_copy(
            src_ref=src, dst_ref=dst, send_sem=send, recv_sem=recv, device_id=to, device_id_type=MESH
        )

    barrier = pltpu.get_barrier_semaphore()

    def greet(to):
        pl.semaphore_signal(barrier, inc=1, device_id=to, device_id_type=MESH)

    for d in range(1, 8):
        greet(at_z(z + d))
        greet(at_frame(lax.rem(f + d, 8)))
    greet(partner)
    greet(cross)
    greet(twin)

    kinds = [hc[i] for i in range(HEADS)]
    n_spatial = HEADS - sum(kinds)
    places, ones = [], 0
    for i, kind in enumerate(kinds):
        places.append((1 - kind) * (i - ones) + kind * (n_spatial + ones))
        ones = ones + kind
    for i in range(HEADS):
        cols = slice(i * HEAD, (i + 1) * HEAD)
        raw[i, 0] = k_in[0, :, cols]
        raw[i, 1] = v_in[0, :, cols]
        raw[i, 2] = q_in[0, :, cols]
    for j in range(HEADS):
        head = sum((places[i] == j).astype(jnp.int32) * i for i in range(1, HEADS))
        st[j] = raw[head]
    pl.semaphore_wait(barrier, 17)

    def mine(a, n):
        return pl.ds(pl.multiple_of(par * HALF + a, HEAD), n)

    def other(a, n):
        return pl.ds(pl.multiple_of((1 - par) * HALF + a, HEAD), n)

    def wz_copy(way, hop):
        sign = 1 if way == 0 else -1
        zs = lax.rem(z - sign * hop + 8, 8)
        cols = mine(0, HALF) if hop < 3 else mine(way * QUARTER, QUARTER)
        dst = wf.at[zs * 2 + xh, c, :, cols]
        src = w_in.at[pl.ds(pl.multiple_of(c * DEEP, DEEP), DEEP), cols] if hop == 0 else dst
        return copy(src, dst, s_wz.at[way, hop], r_wz.at[way, hop], at_z(z + sign + 8))

    def wz_landed(way, hop):
        sign = 1 if way == 0 else -1
        zs = lax.rem(z - sign * (hop + 1) + 8, 8)
        cols = mine(0, HALF) if hop < 3 else mine(way * QUARTER, QUARTER)
        dst = wf.at[zs * 2 + xh, c, :, cols]
        copy(dst, dst, s_wz.at[way, hop], r_wz.at[way, hop], twin).wait_recv()

    def wc_copy(zs, own=False):
        dst = wf.at[zs * 2 + xh, c, :, mine(0, HALF)]
        src = w_in.at[pl.ds(pl.multiple_of(c * DEEP, DEEP), DEEP), mine(0, HALF)] if own else dst
        return copy(src, dst, s_wc.at[zs], r_wc.at[zs], cross)

    def wc_landed(zs):
        dst = wf.at[zs * 2 + 1 - xh, c, :, mine(0, HALF)]
        copy(dst, dst, s_wc.at[zs], r_wc.at[zs], cross).wait_recv()

    def wy_copy(hh, way):
        dst = wf.at[hh, c, :, mine(way * QUARTER, QUARTER)]
        return copy(dst, dst, s_wy.at[way, hh], r_wy.at[way, hh], at_y(1 - 2 * way))

    def wy_landed(hh):
        for way in range(2):
            dst = wf.at[hh, c, :, other(way * QUARTER, QUARTER)]
            copy(dst, dst, s_wy.at[way, hh], r_wy.at[way, hh], twin).wait_recv()

    def wd_copy(hh):
        dst = wf.at[hh, c]
        return copy(dst, dst, s_wd.at[hh], r_wd.at[hh], twin)

    def wd_landed(hh):
        dst = wf.at[hh, 1 - c]
        copy(dst, dst, s_wd.at[hh], r_wd.at[hh], twin).wait_recv()

    def kv_copy(level, i):
        zz = lax.rem(z + around(i), 8)
        there, slot = hosted(spatial, level, zz)
        return there, copy(
            st.at[slot, pl.ds(0, 2)], kv.at[level, xh, z], s_kv.at[level, i], r_kv.at[level, z], at_z(zz)
        )

    def q_copy(level, i):
        zz = lax.rem(z + around(i), 8)
        there, slot = hosted(spatial, level, zz)
        return there, copy(st.at[slot, 2], qb.at[level, z], s_q.at[level, i], r_q.at[level, z], at_z(zz))

    def x_copy(level, zs):
        dst = kv.at[level, xh, zs]
        return copy(dst, dst, s_x.at[level, zs], r_x.at[level, zs], partner)

    def o_copy(level, i):
        zz = lax.rem(z + around(i), 8)
        slot = hosted(spatial, level, z)[1]
        return copy(ost.at[level, zz], at.at[slot], s_o.at[level, i], r_o.at[slot], at_z(zz))

    here = [hosted(spatial, level, z) for level in range(levels)]

    def t_copy(d):
        ff = lax.rem(f + d, 8)
        rows = pl.ds(pl.multiple_of(ff * PART, PART), PART)
        return copy(
            st.at[pl.ds(first_t, temporal), :, rows],
            tb.at[:, :, pl.ds(pl.multiple_of(f * PART, PART), PART)],
            s_t.at[d], r_t.at[f], at_frame(ff),
        )

    def to_copy(d):
        ff = lax.rem(f + d, 8)
        return copy(
            ot.at[:, pl.ds(pl.multiple_of(ff * PART, PART), PART)],
            at.at[pl.ds(spatial, temporal), pl.ds(pl.multiple_of(f * PART, PART), PART)],
            s_to.at[d], r_to.at[f], at_frame(ff),
        )

    for way in range(2):
        wz_copy(way, 0).start()
    wc_copy(z, own=True).start()

    def send_kv(i, carry):
        for level in range(levels):
            there, one = kv_copy(level, i)
            only(there, one.start)
        return carry

    def send_q(i, carry):
        for level in range(levels):
            there, one = q_copy(level, i)
            only(there, one.start)
        return carry

    lax.fori_loop(1, 8, send_kv, 0)
    for level in range(levels):
        there, slot = here[level]

        def keep(level=level, slot=slot):
            kv[level, xh, z] = st[slot, pl.ds(0, 2)]
            qb[level, z] = st[slot, 2]
            x_copy(level, z).start()

        only(there, keep)

    for d in range(1, 8):
        t_copy(d).start()
    own_rows = pl.ds(pl.multiple_of(f * PART, PART), PART)
    tb[:, :, own_rows] = st[pl.ds(first_t, temporal), :, own_rows]
    wf[h, 0] = w_in[pl.ds(0, DEEP), :]
    wf[h, 1] = w_in[pl.ds(DEEP, DEEP), :]
    lax.fori_loop(1, 8, send_q, 0)

    def relay_kv(zs):
        for level in range(levels):
            def go(level=level):
                dst = kv.at[level, xh, zs]
                copy(dst, dst, s_kv.at[level, 0], r_kv.at[level, zs], twin).wait_recv()
                x_copy(level, zs).start()

            only(here[level][0], go)

    def pass_w(zs):
        wc_copy(zs).start()
        for way in range(2):
            wy_copy(zs * 2 + xh, way).start()

    for hop in range(3):
        for way in range(2):
            wz_landed(way, hop)
            wz_copy(way, hop + 1).start()
        for way in range(2):
            zs = lax.rem(z + (hop + 1) * (2 * way - 1) + 8, 8)
            pass_w(zs)
            relay_kv(zs)
    far = lax.rem(z + 4, 8)
    for way in range(2):
        wz_landed(way, 3)
    pass_w(far)
    relay_kv(far)

    for d in range(1, 8):
        ff = lax.rem(f + d, 8)
        dst = tb.at[:, :, pl.ds(pl.multiple_of(ff * PART, PART), PART)]
        copy(dst, dst, s_t.at[d], r_t.at[ff], twin).wait_recv()
    ones_cols = jnp.ones((ROWS, HEAD), jnp.bfloat16)
    lines = lax.broadcasted_iota(jnp.int32, (ROWS, ROWS), 0)
    across = lax.broadcasted_iota(jnp.int32, (ROWS, ROWS), 1)
    same = lax.rem(lines, PART) == lax.rem(across, PART)

    def one_temporal(t, carry):
        scores = jnp.where(same, dot_nt(tb[t, 2], tb[t, 0]), -jnp.inf)
        top = jnp.max(scores, axis=1, keepdims=True)
        weights = jnp.exp2((scores - top) * SCALE).astype(jnp.bfloat16)
        both = jnp.dot(
            weights, jnp.concatenate([tb[t, 1], ones_cols], axis=1), preferred_element_type=jnp.float32
        )
        ot[t] = (both[:, :HEAD] / both[:, HEAD:]).astype(jnp.bfloat16)
        return carry

    lax.fori_loop(0, temporal, one_temporal, 0)
    for d in range(1, 8):
        to_copy(d).start()
    at[pl.ds(spatial, temporal), own_rows] = ot[:, own_rows]

    def partner_kv(zs):
        for level in range(levels):
            def go(level=level):
                dst = kv.at[level, 1 - xh, zs]
                copy(dst, dst, s_x.at[level, 0], r_x.at[level, zs], partner).wait_recv()

            only(here[level][0], go)

    for zs in range(8):
        partner_kv(zs)

    many = 4 * ROWS
    ones_many = jnp.ones((many, HEAD), jnp.bfloat16)

    def attend(level, zs):
        query = qb[level, zs]

        def scores_of(n, top):
            keys = kv[level, lax.div(n, 2), pl.ds(lax.rem(n, 2) * 4, 4), 0].reshape(many, HEAD)
            scores = dot_nt(query, keys)
            sbuf[n] = scores
            for a in range(0, many, HEAD):
                top = jnp.maximum(top, scores[:, a : a + HEAD])
            return top

        top = lax.fori_loop(0, 4, scores_of, jnp.full((ROWS, HEAD), -jnp.inf, jnp.float32))
        top = jnp.max(top, axis=1, keepdims=True)
        acc[...] = jnp.zeros_like(acc)

        def values_of(n, carry):
            weights = jnp.exp2((sbuf[n] - top) * SCALE).astype(jnp.bfloat16)
            vals = kv[level, lax.div(n, 2), pl.ds(lax.rem(n, 2) * 4, 4), 1].reshape(many, HEAD)
            acc[...] += jnp.dot(
                weights, jnp.concatenate([vals, ones_many], axis=1), preferred_element_type=jnp.float32
            )
            return carry

        lax.fori_loop(0, 4, values_of, 0)
        return (acc[:, :HEAD] / acc[:, HEAD:]).astype(jnp.bfloat16)

    def chunk(i, carry):
        zs = lax.rem(z + around(i), 8)
        for level in range(levels):
            there, slot = here[level]

            def go(level=level, slot=slot):
                @pl.when(i > 0)
                def _():
                    dst = qb.at[level, zs]
                    copy(dst, dst, s_q.at[level, 0], r_q.at[level, zs], twin).wait_recv()

                ost[level, zs] = attend(level, zs)

                @pl.when(i > 0)
                def _():
                    o_copy(level, i).start()

                @pl.when(i == 0)
                def _():
                    at[slot] = ost[level, zs]

            only(there, go)
        wc_landed(zs)
        for way in range(2):
            wy_copy(zs * 2 + 1 - xh, way).start()

        @pl.when(i > 0)
        def _():
            wy_landed(zs * 2 + xh)
            wd_copy(zs * 2 + xh).start()

        return carry

    lax.fori_loop(0, 8, chunk, 0)

    def last_w(i, carry):
        zs = lax.rem(z + around(i), 8)
        wy_landed(zs * 2 + 1 - xh)
        wd_copy(zs * 2 + 1 - xh).start()
        return carry

    lax.fori_loop(0, 8, last_w, 0)

    for d in range(1, 8):
        ff = lax.rem(f + d, 8)
        dst = at.at[pl.ds(spatial, temporal), pl.ds(pl.multiple_of(ff * PART, PART), PART)]
        copy(dst, dst, s_to.at[d], r_to.at[ff], twin).wait_recv()

    def o_landed(i, carry):
        zz = lax.rem(z + around(i), 8)
        for level in range(levels):
            there, slot = hosted(spatial, level, zz)

            def go(level=level, slot=slot):
                dst = at.at[slot]
                copy(dst, dst, s_o.at[level, 0], r_o.at[slot], twin).wait_recv()

            only(there, go)
        return carry

    lax.fori_loop(1, 8, o_landed, 0)
    for i in range(HEADS):
        where_at = places[i] + kinds[i] * (spatial - first_t)
        cat[:, i * HEAD : (i + 1) * HEAD] = at[where_at]

    def wd_wait(hh, carry):
        pl.when(hh != h)(lambda: wd_landed(hh))
        return carry

    lax.fori_loop(0, HEADS, wd_wait, 0)

    def project(n, carry):
        cols = pl.ds(pl.multiple_of(n * 512, 512), 512)
        out[0, :, cols] = jnp.dot(
            cat[...], wf[:, :, :, cols].reshape(HEADS * HEAD, 512), preferred_element_type=jnp.float32
        ).astype(jnp.bfloat16)
        return carry

    lax.fori_loop(0, WIDE // 512, project, 0)

    def sent(i, carry):
        zz = lax.rem(z + around(i), 8)
        for level in range(levels):
            for one_copy in (kv_copy, q_copy):
                there, one = one_copy(level, i)
                only(there, one.wait_send)
            only(here[level][0], lambda level=level: o_copy(level, i).wait_send())
        wc_copy(zz).wait_send()
        for way in range(2):
            wy_copy(zz * 2 + xh, way).wait_send()
        wd_copy(zz * 2 + xh).wait_send()
        return carry

    lax.fori_loop(1, 8, sent, 0)
    wc_copy(z).wait_send()
    for way in range(2):
        for hop in range(4):
            wz_copy(way, hop).wait_send()

    def sent_more(zs, carry):
        for level in range(levels):
            only(here[level][0], lambda level=level: x_copy(level, zs).wait_send())
        for way in range(2):
            wy_copy(zs * 2 + 1 - xh, way).wait_send()
        wd_copy(zs * 2 + 1 - xh).wait_send()
        return carry

    lax.fori_loop(0, 8, sent_more, 0)
    for d in range(1, 8):
        t_copy(d).wait_send()
        to_copy(d).wait_send()


def layer(number, spatial, temporal, head_class, queries, keys, values, w_out):
    levels = 1 if spatial <= 8 else 2
    bf16, f32, dma = jnp.bfloat16, jnp.float32, pltpu.SemaphoreType.DMA
    whole = pl.BlockSpec(memory_space=pltpu.VMEM)
    return pl.pallas_call(
        functools.partial(kernel, spatial, temporal),
        out_shape=jax.ShapeDtypeStruct((1, ROWS, WIDE), bf16),
        in_specs=[pl.BlockSpec(memory_space=pltpu.SMEM)] + [whole] * 4,
        out_specs=whole,
        scratch_shapes=[
            pltpu.VMEM((HEADS, 3, ROWS, HEAD), bf16),
            pltpu.VMEM((HEADS, 3, ROWS, HEAD), bf16),
            pltpu.VMEM((levels, 2, 8, 2, ROWS, HEAD), bf16),
            pltpu.VMEM((levels, 8, ROWS, HEAD), bf16),
            pltpu.VMEM((temporal, 3, ROWS, HEAD), bf16),
            pltpu.VMEM((temporal, ROWS, HEAD), bf16),
            pltpu.VMEM((levels, 8, ROWS, HEAD), bf16),
            pltpu.VMEM((spatial + temporal, ROWS, HEAD), bf16),
            pltpu.VMEM((ROWS, HEADS * HEAD), bf16),
            pltpu.VMEM((HEADS, 2, DEEP, WIDE), bf16),
            pltpu.VMEM((4, ROWS, 4 * ROWS), f32),
            pltpu.VMEM((ROWS, 2 * HEAD), f32),
        ]
        + [dma((levels, 8))] * 7 + [dma((HEADS,))]
        + [dma((8,))] * 4
        + [dma((2, 4))] * 2 + [dma((8,))] * 2 + [dma((2, HEADS))] * 2 + [dma((HEADS,))] * 2,
        compiler_params=pltpu.CompilerParams(
            collective_id=number, has_side_effects=True, vmem_limit_bytes=56 * 2**20
        ),
        name=f"layer_{spatial}",
    )(head_class, queries, keys, values, w_out)


def on_device(queries, keys, values, head_class, w_out):
    n_spatial = jnp.sum((head_class == 0).astype(jnp.int32))
    plans, below = [], 0
    for number, spatial in enumerate(PLANS):
        plans.append(functools.partial(layer, number, spatial, HEADS - below - 1))
        below = spatial
    which = sum((n_spatial > spatial).astype(jnp.int32) for spatial in PLANS[:-1])
    operands = (head_class, queries, keys, values, w_out)
    return lax.switch(which, plans, *operands)


def solution(mesh):
    placed = (
        P(("rep", "frame"), "head", None),
        P(("rep", "frame"), "head", None),
        P(("rep", "frame"), "head", None),
        P(),
        P("head", None),
    )
    return jax.shard_map(
        on_device,
        mesh=mesh,
        in_specs=placed,
        out_specs=P(("rep", "frame"), "head", None),
        check_vma=False,
    )
```

```python
import functools

import jax
import jax.numpy as jnp
from jax import lax
from jax.experimental import pallas as pl
from jax.experimental.pallas import tpu as pltpu
from jax.sharding import PartitionSpec as P

HEADS = 16
HEAD = 128
ROWS = 256
PART = 32
FRAMES = 8
WIDE = 3072
HALF = WIDE // 2
QUARTER = WIDE // 4
DEEP = 64
SCALE = HEAD**-0.5 * 1.4426950408889634
MESH = pl.DeviceIdType.MESH

PLANS = (4, 5, 6, 7, 8, 9, 10, 11, 12, 15)


ORDER = (
    [("own", 0), ("kv", 0), ("kv", 1), ("kv", 2), ("stage", 0)]
    + [("t", i) for i in range(1, 5)]
    + [("kv", i) for i in range(3, 7)]
    + [("t", i) for i in range(5, 8)]
    + [("hop", 0), ("pass", 1), ("pass", 2), ("hop", 1), ("pass", 3), ("pass", 4), ("relay", 0), ("relay", 1)]
    + [("hop", 2), ("pass", 5), ("pass", 6), ("q", 0), ("relay", 2), ("relay", 3), ("temporal", 0)]
    + [("hop", 3), ("pass", 7), ("relay", 4), ("relay", 5), ("relay", 6), ("across", 0), ("across", 1)]
)


def dot_nt(a, b):
    return lax.dot_general(a, b, (((1,), (1,)), ((), ())), preferred_element_type=jnp.float32)


def rem(a, n):
    return a & (n - 1)


def div(a, n):
    return a >> (n.bit_length() - 1)


def near(i):
    return 8 + div(i + 1, 2) * (2 * rem(i, 2) - 1)


def around(i, c):
    return 8 + (near(7 - i) - 8) * (1 - 2 * c)


def hosts_of(count):
    return [(k * 8) // count for k in range(count)]


def hosted(spatial, level, zz):
    count = min(spatial, 8) if level == 0 else spatial - 8
    if count == 8:
        return None, zz + 8 * level
    hosts = hosts_of(count)
    there = sum((zz == k).astype(jnp.int32) for k in hosts)
    slot = sum((zz > k).astype(jnp.int32) for k in hosts)
    return there == 1, slot + 8 * level


def only(condition, body):
    if condition is None:
        body()
    else:
        pl.when(condition)(body)


def kernel(
    spatial, temporal, hc, q_in, k_in, v_in, w_in, out,
    raw, st, stt, kv, qb, tb, ot, ost, at, cat, wf, sbuf, acc, tops,
    s_kv, r_kv, s_q, r_q, s_x, r_x, s_o, r_o, s_t, r_t, s_to, r_to,
    s_wz, r_wz, s_wc, r_wc, s_wy, r_wy, s_wd, r_wd,
):
    levels = 1 if spatial <= 8 else 2
    first_t = HEADS - temporal
    f, h, c = lax.axis_index("frame"), lax.axis_index("head"), lax.axis_index("rep")
    xl, y = div(f, 4), rem(f, 4)
    z, xh = div(h, 2), rem(h, 2)
    par = rem(y, 2)

    def at_z(zz):
        return (f, rem(zz, 8) * 2 + xh, c)

    def at_frame(ff):
        return (ff, h, c)

    def at_y(step):
        return (xl * 4 + rem(y + step + 4, 4), h, c)

    partner = (f, z * 2 + 1 - xh, c)
    cross = ((1 - xl) * 4 + y, z * 2 + 1 - xh, c)
    twin = (f, h, 1 - c)

    def copy(src, dst, send, recv, to):
        return pltpu.make_async_remote_copy(
            src_ref=src, dst_ref=dst, send_sem=send, recv_sem=recv, device_id=to, device_id_type=MESH
        )

    barrier = pltpu.get_barrier_semaphore()

    def greet(to):
        pl.semaphore_signal(barrier, inc=1, device_id=to, device_id_type=MESH)

    for d in range(1, 8):
        greet(at_z(z + d))
        greet(at_frame(rem(f + d, 8)))
    greet(partner)
    greet(cross)
    greet(twin)

    kinds = [hc[i] for i in range(HEADS)]
    n_spatial = HEADS - sum(kinds)
    places, ones = [], 0
    for i, kind in enumerate(kinds):
        places.append((1 - kind) * (i - ones) + kind * (n_spatial + ones))
        ones = ones + kind
    pl.semaphore_wait(barrier, 17)

    def mine(a, n):
        return pl.ds(pl.multiple_of(par * HALF + a, HEAD), n)

    def other(a, n):
        return pl.ds(pl.multiple_of((1 - par) * HALF + a, HEAD), n)

    def wz_copy(way, hop):
        sign = 1 if way == 0 else -1
        zs = rem(z - sign * hop + 8, 8)
        cols = mine(0, HALF) if hop < 3 else mine(way * QUARTER, QUARTER)
        dst = wf.at[zs * 2 + xh, c, :, cols]
        src = w_in.at[pl.ds(pl.multiple_of(c * DEEP, DEEP), DEEP), cols] if hop == 0 else dst
        return copy(src, dst, s_wz.at[way, hop], r_wz.at[way, hop], at_z(z + sign + 8))

    def wz_landed(way, hop):
        sign = 1 if way == 0 else -1
        zs = rem(z - sign * (hop + 1) + 8, 8)
        cols = mine(0, HALF) if hop < 3 else mine(way * QUARTER, QUARTER)
        dst = wf.at[zs * 2 + xh, c, :, cols]
        copy(dst, dst, s_wz.at[way, hop], r_wz.at[way, hop], twin).wait_recv()

    def wc_copy(zs, own=False):
        dst = wf.at[zs * 2 + xh, c, :, mine(0, HALF)]
        src = w_in.at[pl.ds(pl.multiple_of(c * DEEP, DEEP), DEEP), mine(0, HALF)] if own else dst
        return copy(src, dst, s_wc.at[zs], r_wc.at[zs], cross)

    def wc_landed(zs):
        dst = wf.at[zs * 2 + 1 - xh, c, :, mine(0, HALF)]
        copy(dst, dst, s_wc.at[zs], r_wc.at[zs], cross).wait_recv()

    def wy_copy(hh, way):
        dst = wf.at[hh, c, :, mine(way * QUARTER, QUARTER)]
        return copy(dst, dst, s_wy.at[way, hh], r_wy.at[way, hh], at_y(1 - 2 * way))

    def wy_landed(hh):
        for way in range(2):
            dst = wf.at[hh, c, :, other(way * QUARTER, QUARTER)]
            copy(dst, dst, s_wy.at[way, hh], r_wy.at[way, hh], twin).wait_recv()

    def wd_copy(hh, half):
        dst = wf.at[hh, c, :, (mine, other)[half](0, HALF)]
        return copy(dst, dst, s_wd.at[half, hh], r_wd.at[half, hh], twin)

    def wd_landed(hh):
        for half in range(2):
            dst = wf.at[hh, 1 - c, :, (mine, other)[half](0, HALF)]
            copy(dst, dst, s_wd.at[half, hh], r_wd.at[half, hh], twin).wait_recv()

    def kv_copy(level, i):
        zz = rem(z + around(i, c), 8)
        there, slot = hosted(spatial, level, zz)
        return there, copy(
            st.at[slot, pl.ds(0, 2)], kv.at[level, xh, z], s_kv.at[level, i], r_kv.at[level, z], at_z(zz)
        )

    def q_copy(level, i):
        zz = rem(z + around(i, c), 8)
        there, slot = hosted(spatial, level, zz)
        return there, copy(st.at[slot, 2], qb.at[level, z], s_q.at[level, i], r_q.at[level, z], at_z(zz))

    def x_copy(level, zs):
        dst = kv.at[level, xh, zs]
        return copy(dst, dst, s_x.at[level, zs], r_x.at[level, zs], partner)

    def o_copy(level, i):
        zz = rem(z + around(i, c), 8)
        slot = here[0][1] if levels == 1 else here[0][1] + level * (here[1][1] - here[0][1])
        return copy(ost.at[level, zz], at.at[slot], s_o.at[level, i], r_o.at[slot], at_z(zz))

    here = [hosted(spatial, level, z) for level in range(levels)]

    def t_copy(d):
        ff = rem(f + d, 8)
        rows = pl.ds(pl.multiple_of(ff * PART, PART), PART)
        return copy(
            stt.at[:, :, rows],
            tb.at[:, :, pl.ds(pl.multiple_of(f * PART, PART), PART)],
            s_t.at[d], r_t.at[f], at_frame(ff),
        )

    def to_copy(d):
        ff = rem(f + d, 8)
        return copy(
            ot.at[:, pl.ds(pl.multiple_of(ff * PART, PART), PART)],
            at.at[pl.ds(spatial, temporal), pl.ds(pl.multiple_of(f * PART, PART), PART)],
            s_to.at[d], r_to.at[f], at_frame(ff),
        )

    for way in range(2):
        wz_copy(way, 0).start()
    wc_copy(z, own=True).start()

    def held_by(j):
        return sum((places[i] == j).astype(jnp.int32) * i for i in range(1, HEADS))

    def split(i, carry):
        cols = pl.ds(pl.multiple_of(i * HEAD, HEAD), HEAD)
        raw[i, 0] = k_in[0, :, cols]
        raw[i, 1] = v_in[0, :, cols]
        raw[i, 2] = q_in[0, :, cols]
        return carry

    def stage_spatial(j, carry):
        head = held_by(j)
        st[j, 0] = raw[head, 0]
        for a in range(0, ROWS, HEAD):
            st[j, 1, a : a + HEAD] = raw[head, 1, a : a + HEAD].T
        st[j, 2] = raw[head, 2]
        return carry

    def stage_temporal(t, carry):
        stt[t] = raw[held_by(first_t + t)]
        return carry

    lax.fori_loop(0, HEADS, split, 0)
    lax.fori_loop(0, spatial, stage_spatial, 0)

    def send_kv(i):
        for level in range(levels):
            there, one = kv_copy(level, i)
            only(there, one.start)

    def send_q(i, carry):
        for level in range(levels):
            there, one = q_copy(level, i)
            only(there, one.start)
        return carry

    def relay_kv(zs):
        for level in range(levels):
            def go(level=level):
                dst = kv.at[level, xh, zs]
                copy(dst, dst, s_kv.at[level, 0], r_kv.at[level, zs], twin).wait_recv()
                x_copy(level, zs).start()

            only(here[level][0], go)

    def pass_w(zs):
        wc_copy(zs).start()
        for way in range(2):
            wy_copy(zs * 2 + xh, way).start()
        wd_copy(zs * 2 + xh, 0).start()

    def at_step(i):
        return rem(z + around(i, c), 8)

    def near_step(i):
        return rem(z + near(i), 8)

    def keep_own():
        for level in range(levels):
            there, slot = here[level]

            def keep(level=level, slot=slot):
                kv[level, xh, z] = st[slot, pl.ds(0, 2)]
                qb[level, z] = st[slot, 2]
                x_copy(level, z).start()

            only(there, keep)
        wf[h, 0] = w_in[pl.ds(0, DEEP), :]
        wf[h, 1] = w_in[pl.ds(DEEP, DEEP), :]

    own_rows = pl.ds(pl.multiple_of(f * PART, PART), PART)

    def hop_w(hop):
        for way in range(2):
            wz_landed(way, hop)
            if hop < 3:
                wz_copy(way, hop + 1).start()

    ones_cols = jnp.ones((ROWS, HEAD), jnp.bfloat16)
    lines = lax.broadcasted_iota(jnp.int32, (ROWS, ROWS), 0)
    across = lax.broadcasted_iota(jnp.int32, (ROWS, ROWS), 1)
    same = rem(lines, PART) == rem(across, PART)

    def some_temporal(first, count):
        ts = [first + a for a in range(count)]
        scores = [jnp.where(same, dot_nt(tb[t, 2], tb[t, 0]), -jnp.inf) for t in ts]
        tops = [jnp.max(one, axis=1, keepdims=True) for one in scores]
        weights = [jnp.exp2((one - top) * SCALE).astype(jnp.bfloat16) for one, top in zip(scores, tops)]
        for t, one in zip(ts, weights):
            both = jnp.dot(
                one, jnp.concatenate([tb[t, 1], ones_cols], axis=1), preferred_element_type=jnp.float32
            )
            ot[t] = (both[:, :HEAD] / both[:, HEAD:]).astype(jnp.bfloat16)

    def attend_temporal():
        for d in range(1, 8):
            ff = rem(f + d, 8)
            dst = tb.at[:, :, pl.ds(pl.multiple_of(ff * PART, PART), PART)]
            copy(dst, dst, s_t.at[d], r_t.at[ff], twin).wait_recv()
        tb[:, :, own_rows] = stt[:, :, own_rows]
        lax.fori_loop(0, temporal // 3, lambda g, carry: some_temporal(3 * g, 3), None)
        if temporal % 3:
            some_temporal(temporal - temporal % 3, temporal % 3)
        for d in range(1, 8):
            to_copy(d).start()
        at[pl.ds(spatial, temporal), own_rows] = ot[:, own_rows]

    def w_step(i):
        zs = near_step(i)
        wc_landed(zs)
        for way in range(2):
            wy_copy(zs * 2 + 1 - xh, way).start()
        wd_copy(zs * 2 + 1 - xh, 0).start()

        @pl.when(i > 0)
        def _():
            wy_landed(zs * 2 + xh)
            wd_copy(zs * 2 + xh, 1).start()
            before = near_step(i - 1) * 2 + 1 - xh
            wy_landed(before)
            wd_copy(before, 1).start()

    doings = {
        "kv": send_kv,
        "t": lambda d: t_copy(d).start(),
        "q": lambda i: lax.fori_loop(0, 7, send_q, 0),
        "own": lambda i: keep_own(),
        "stage": lambda i: lax.fori_loop(0, temporal, stage_temporal, 0),
        "hop": hop_w,
        "pass": lambda i: pass_w(near_step(i)),
        "relay": lambda i: relay_kv(at_step(i)),
        "temporal": lambda i: attend_temporal(),
        "across": w_step,
    }
    early = 0
    for what, number in ORDER:
        doings[what](number)
        early += what == "across"

    def partner_kv(zs):
        for level in range(levels):
            def go(level=level):
                dst = kv.at[level, 1 - xh, zs]
                copy(dst, dst, s_x.at[level, 0], r_x.at[level, zs], partner).wait_recv()

            only(here[level][0], go)

    for zs in range(8):
        partner_kv(zs)

    block = 2 * ROWS
    blocks = HEADS * ROWS // block
    ones_rows = jnp.ones((16, block), jnp.bfloat16)
    lowest = jnp.full((32, ROWS), -jnp.inf, jnp.float32)

    def scores_of(level, zs, n, slot):
        keys = kv[level, n // 4, pl.ds(2 * (n % 4), 2), 0].reshape(block, HEAD)
        scores = dot_nt(keys, qb[level, zs])
        sbuf[slot * blocks + n] = scores
        return jnp.max(scores.reshape(block // 32, 32, ROWS), axis=0)

    def values_of(level, n):
        parts = [
            kv[level, n // 4, 2 * (n % 4) + a, 1, b : b + HEAD] for a in range(2) for b in range(0, ROWS, HEAD)
        ]
        return jnp.concatenate([jnp.concatenate(parts, axis=1), ones_rows], axis=0)

    def first_scores(level):
        def some(m, top):
            for a in range(4):
                top = jnp.maximum(top, scores_of(level, at_step(0), 4 * m + a, 0))
            return top

        tops[0] = jnp.max(lax.fori_loop(0, blocks // 4, some, lowest), axis=0, keepdims=True)

    def attend(level, zs, later, slot):
        top, next_top = tops[slot], lowest
        for n in range(blocks):
            weights = jnp.exp2((sbuf[slot * blocks + n] - top) * SCALE).astype(jnp.bfloat16)
            part = jnp.dot(values_of(level, n), weights, preferred_element_type=jnp.float32)
            next_top = jnp.maximum(next_top, scores_of(level, later, n, 1 - slot))
            if n == 0:
                acc[...] = part
            else:
                acc[...] += part
        tops[1 - slot] = jnp.max(next_top, axis=0, keepdims=True)
        return (acc[:HEAD] / acc[HEAD : HEAD + 1]).T.astype(jnp.bfloat16)

    def spatial_chunk(level, slot_here, i):
        zs, later = at_step(i), at_step(rem(i + 1, 8))

        @pl.when(i == 0)
        def _():
            dst = qb.at[level, zs]
            copy(dst, dst, s_q.at[level, 0], r_q.at[level, zs], twin).wait_recv()
            first_scores(level)

        @pl.when(i < 6)
        def _():
            dst = qb.at[level, later]
            copy(dst, dst, s_q.at[level, 0], r_q.at[level, later], twin).wait_recv()

        ost[level, zs] = attend(level, zs, later, rem(i, 2))

        @pl.when(i < 7)
        def _():
            o_copy(level, i).start()

        @pl.when(i == 7)
        def _():
            at[slot_here] = ost[level, zs]

    def step(n, carry):
        level, i = div(n, 8), rem(n, 8)
        if levels == 1:
            there, slot_here = here[0]
            level = 0
        else:
            there = (level == 0) | here[1][0]
            slot_here = here[0][1] + level * (here[1][1] - here[0][1])
        only(there, functools.partial(spatial_chunk, level, slot_here, i))
        pl.when(n < 8 - early)(lambda: w_step(n + early))
        return carry

    lax.fori_loop(0, 8 * levels, step, 0)
    last = near_step(7) * 2 + 1 - xh
    wy_landed(last)
    wd_copy(last, 1).start()

    for d in range(1, 8):
        ff = rem(f + d, 8)
        dst = at.at[pl.ds(spatial, temporal), pl.ds(pl.multiple_of(ff * PART, PART), PART)]
        copy(dst, dst, s_to.at[d], r_to.at[ff], twin).wait_recv()

    def o_landed(i, carry):
        zz = rem(z + around(i, c), 8)
        for level in range(levels):
            there, slot = hosted(spatial, level, zz)

            def go(level=level, slot=slot):
                dst = at.at[slot]
                copy(dst, dst, s_o.at[level, 0], r_o.at[slot], twin).wait_recv()

            only(there, go)
        return carry

    lax.fori_loop(0, 7, o_landed, 0)
    for i in range(HEADS):
        where_at = places[i] + kinds[i] * (spatial - first_t)
        cat[:, i * HEAD : (i + 1) * HEAD] = at[where_at]

    def wd_wait(hh, carry):
        pl.when(hh != h)(lambda: wd_landed(hh))
        return carry

    lax.fori_loop(0, HEADS, wd_wait, 0)

    def project(n, carry):
        cols = pl.ds(pl.multiple_of(n * 512, 512), 512)
        out[0, :, cols] = jnp.dot(
            cat[...], wf[:, :, :, cols].reshape(HEADS * HEAD, 512), preferred_element_type=jnp.float32
        ).astype(jnp.bfloat16)
        return carry

    lax.fori_loop(0, WIDE // 512, project, 0)

    def sent(i, carry):
        zz = rem(z + around(i, c), 8)
        for level in range(levels):
            for one_copy in (kv_copy, q_copy):
                there, one = one_copy(level, i)
                only(there, one.wait_send)
            only(here[level][0], lambda level=level: o_copy(level, i).wait_send())
        wc_copy(zz).wait_send()
        for way in range(2):
            wy_copy(zz * 2 + xh, way).wait_send()
            wd_copy(zz * 2 + xh, way).wait_send()
        return carry

    lax.fori_loop(0, 7, sent, 0)
    wc_copy(z).wait_send()
    for way in range(2):
        for hop in range(4):
            wz_copy(way, hop).wait_send()

    def sent_more(zs, carry):
        for level in range(levels):
            only(here[level][0], lambda level=level: x_copy(level, zs).wait_send())
        for way in range(2):
            wy_copy(zs * 2 + 1 - xh, way).wait_send()
            wd_copy(zs * 2 + 1 - xh, way).wait_send()
        return carry

    lax.fori_loop(0, 8, sent_more, 0)
    for d in range(1, 8):
        t_copy(d).wait_send()
        to_copy(d).wait_send()


def layer(number, spatial, temporal, head_class, queries, keys, values, w_out):
    levels = 1 if spatial <= 8 else 2
    bf16, f32, dma = jnp.bfloat16, jnp.float32, pltpu.SemaphoreType.DMA
    whole = pl.BlockSpec(memory_space=pltpu.VMEM)
    return pl.pallas_call(
        functools.partial(kernel, spatial, temporal),
        out_shape=jax.ShapeDtypeStruct((1, ROWS, WIDE), bf16),
        in_specs=[pl.BlockSpec(memory_space=pltpu.SMEM)] + [whole] * 4,
        out_specs=whole,
        scratch_shapes=[
            pltpu.VMEM((HEADS, 3, ROWS, HEAD), bf16),
            pltpu.VMEM((spatial, 3, ROWS, HEAD), bf16),
            pltpu.VMEM((temporal, 3, ROWS, HEAD), bf16),
            pltpu.VMEM((levels, 2, 8, 2, ROWS, HEAD), bf16),
            pltpu.VMEM((levels, 8, ROWS, HEAD), bf16),
            pltpu.VMEM((temporal, 3, ROWS, HEAD), bf16),
            pltpu.VMEM((temporal, ROWS, HEAD), bf16),
            pltpu.VMEM((levels, 8, ROWS, HEAD), bf16),
            pltpu.VMEM((spatial + temporal, ROWS, HEAD), bf16),
            pltpu.VMEM((ROWS, HEADS * HEAD), bf16),
            pltpu.VMEM((HEADS, 2, DEEP, WIDE), bf16),
            pltpu.VMEM((HEADS, 2 * ROWS, ROWS), f32),
            pltpu.VMEM((HEAD + 16, ROWS), f32),
            pltpu.VMEM((2, 1, ROWS), f32),
        ]
        + [dma((levels, 8))] * 7 + [dma((HEADS,))]
        + [dma((8,))] * 4
        + [dma((2, 4))] * 2 + [dma((8,))] * 2 + [dma((2, HEADS))] * 4,
        compiler_params=pltpu.CompilerParams(
            collective_id=number, has_side_effects=True, vmem_limit_bytes=56 * 2**20
        ),
        name=f"layer_{spatial}",
    )(head_class, queries, keys, values, w_out)


def on_device(queries, keys, values, head_class, w_out):
    n_spatial = jnp.sum((head_class == 0).astype(jnp.int32))
    plans, below = [], 0
    for number, spatial in enumerate(PLANS):
        plans.append(functools.partial(layer, number, spatial, HEADS - below - 1))
        below = spatial
    which = sum((n_spatial > spatial).astype(jnp.int32) for spatial in PLANS[:-1])
    operands = (head_class, queries, keys, values, w_out)
    return lax.switch(which, plans, *operands)


def solution(mesh):
    placed = (
        P(("rep", "frame"), "head", None),
        P(("rep", "frame"), "head", None),
        P(("rep", "frame"), "head", None),
        P(),
        P("head", None),
    )
    return jax.shard_map(
        on_device,
        mesh=mesh,
        in_specs=placed,
        out_specs=P(("rep", "frame"), "head", None),
        check_vma=False,
    )
```

```python
import functools

import jax
import jax.numpy as jnp
from jax import lax
from jax.experimental import pallas as pl
from jax.experimental.pallas import tpu as pltpu
from jax.sharding import PartitionSpec as P

HEADS = 16
HEAD = 128
ROWS = 256
PART = 32
FRAMES = 8
WIDE = 3072
HALF = WIDE // 2
QUARTER = WIDE // 4
DEEP = 64
SCALE = HEAD**-0.5 * 1.4426950408889634
MESH = pl.DeviceIdType.MESH

PLANS = (5, 6, 7, 8, 9, 10, 12, 15)


ORDER = (
    [("own", 0), ("kv", 0), ("kv", 1), ("kv", 2), ("stage", 0)]
    + [("t", i) for i in range(1, 5)]
    + [("kv", i) for i in range(3, 7)]
    + [("t", i) for i in range(5, 8)]
    + [("hop", 0), ("pass", 1), ("pass", 2), ("hop", 1), ("pass", 3), ("pass", 4), ("relay", 0), ("relay", 1)]
    + [("hop", 2), ("pass", 5), ("pass", 6), ("q", 0), ("relay", 2), ("relay", 3), ("temporal", 0)]
    + [("hop", 3), ("pass", 7), ("relay", 4), ("relay", 5), ("relay", 6), ("across", 0), ("across", 1)]
)


def dot_nt(a, b):
    return lax.dot_general(a, b, (((1,), (1,)), ((), ())), preferred_element_type=jnp.float32)


def rem(a, n):
    return a & (n - 1)


def div(a, n):
    return a >> (n.bit_length() - 1)


def near(i):
    return 8 + div(i + 1, 2) * (2 * rem(i, 2) - 1)


def around(i, c):
    return 8 + (near(7 - i) - 8) * (1 - 2 * c)


def hosts_of(count):
    return [(k * 8) // count for k in range(count)]


def levels_of(spatial):
    return 1 if spatial <= 8 else 2 + (spatial - 9) // 4


def hosted(spatial, level, zz):
    if level > 0:
        return rem(zz, 4) < spatial - 4 - 4 * level, 4 + 4 * level + rem(zz, 4)
    if spatial >= 8:
        return None, zz
    hosts = hosts_of(spatial)
    there = sum((zz == k).astype(jnp.int32) for k in hosts)
    return there == 1, sum((zz > k).astype(jnp.int32) for k in hosts)


def served(level, source, host):
    if level == 0:
        return None
    return rem(source - host + 9, 8) < 4


def both(a, b):
    return b if a is None else a if b is None else a & b


def shared(i):
    early = 1 - div(i, 2)
    return early * (2 - i) + (1 - early) * rem(i + 5, 8)


def only(condition, body):
    if condition is None:
        body()
    else:
        pl.when(condition)(body)


def kernel(
    spatial, temporal, hc, q_in, k_in, v_in, w_in, out,
    raw, st, stt, kv, qb, tb, ot, ost, at, cat, wf, sbuf, acc, tops,
    s_kv, r_kv, s_q, r_q, s_x, r_x, s_o, r_o, s_t, r_t, s_to, r_to,
    s_wz, r_wz, s_wc, r_wc, s_wy, r_wy, s_wd, r_wd,
):
    levels = levels_of(spatial)
    first_t = HEADS - temporal
    f, h, c = lax.axis_index("frame"), lax.axis_index("head"), lax.axis_index("rep")
    xl, y = div(f, 4), rem(f, 4)
    z, xh = div(h, 2), rem(h, 2)
    par = rem(y, 2)

    def at_z(zz):
        return (f, rem(zz, 8) * 2 + xh, c)

    def at_frame(ff):
        return (ff, h, c)

    def at_y(step):
        return (xl * 4 + rem(y + step + 4, 4), h, c)

    partner = (f, z * 2 + 1 - xh, c)
    cross = ((1 - xl) * 4 + y, z * 2 + 1 - xh, c)
    twin = (f, h, 1 - c)

    def copy(src, dst, send, recv, to):
        return pltpu.make_async_remote_copy(
            src_ref=src, dst_ref=dst, send_sem=send, recv_sem=recv, device_id=to, device_id_type=MESH
        )

    barrier = pltpu.get_barrier_semaphore()

    def greet(to):
        pl.semaphore_signal(barrier, inc=1, device_id=to, device_id_type=MESH)

    for d in range(1, 8):
        greet(at_z(z + d))
        greet(at_frame(rem(f + d, 8)))
    greet(partner)
    greet(cross)
    greet(twin)

    kinds = [hc[i] for i in range(HEADS)]
    n_spatial = HEADS - sum(kinds)
    places, ones = [], 0
    for i, kind in enumerate(kinds):
        places.append((1 - kind) * (i - ones) + kind * (n_spatial + ones))
        ones = ones + kind
    pl.semaphore_wait(barrier, 17)

    def mine(a, n):
        return pl.ds(pl.multiple_of(par * HALF + a, HEAD), n)

    def other(a, n):
        return pl.ds(pl.multiple_of((1 - par) * HALF + a, HEAD), n)

    def wz_copy(way, hop):
        sign = 1 if way == 0 else -1
        zs = rem(z - sign * hop + 8, 8)
        cols = mine(0, HALF) if hop < 3 else mine(way * QUARTER, QUARTER)
        dst = wf.at[zs * 2 + xh, c, :, cols]
        src = w_in.at[pl.ds(pl.multiple_of(c * DEEP, DEEP), DEEP), cols] if hop == 0 else dst
        return copy(src, dst, s_wz.at[way, hop], r_wz.at[way, hop], at_z(z + sign + 8))

    def wz_landed(way, hop):
        sign = 1 if way == 0 else -1
        zs = rem(z - sign * (hop + 1) + 8, 8)
        cols = mine(0, HALF) if hop < 3 else mine(way * QUARTER, QUARTER)
        dst = wf.at[zs * 2 + xh, c, :, cols]
        copy(dst, dst, s_wz.at[way, hop], r_wz.at[way, hop], twin).wait_recv()

    def wc_copy(zs, own=False):
        dst = wf.at[zs * 2 + xh, c, :, mine(0, HALF)]
        src = w_in.at[pl.ds(pl.multiple_of(c * DEEP, DEEP), DEEP), mine(0, HALF)] if own else dst
        return copy(src, dst, s_wc.at[zs], r_wc.at[zs], cross)

    def wc_landed(zs):
        dst = wf.at[zs * 2 + 1 - xh, c, :, mine(0, HALF)]
        copy(dst, dst, s_wc.at[zs], r_wc.at[zs], cross).wait_recv()

    def wy_copy(hh, way):
        dst = wf.at[hh, c, :, mine(way * QUARTER, QUARTER)]
        return copy(dst, dst, s_wy.at[way, hh], r_wy.at[way, hh], at_y(1 - 2 * way))

    def wy_landed(hh):
        for way in range(2):
            dst = wf.at[hh, c, :, other(way * QUARTER, QUARTER)]
            copy(dst, dst, s_wy.at[way, hh], r_wy.at[way, hh], twin).wait_recv()

    def wd_copy(hh, half):
        dst = wf.at[hh, c, :, (mine, other)[half](0, HALF)]
        return copy(dst, dst, s_wd.at[half, hh], r_wd.at[half, hh], twin)

    def wd_landed(hh):
        for half in range(2):
            dst = wf.at[hh, 1 - c, :, (mine, other)[half](0, HALF)]
            copy(dst, dst, s_wd.at[half, hh], r_wd.at[half, hh], twin).wait_recv()

    def kv_copy(level, i):
        zz = rem(z + around(i, c), 8)
        there, slot = hosted(spatial, level, zz)
        return there, copy(
            st.at[slot, pl.ds(0, 2)], kv.at[level, xh, z], s_kv.at[level, i], r_kv.at[level, z], at_z(zz)
        )

    def q_copy(level, i):
        zz = rem(z + around(i, c), 8)
        there, slot = hosted(spatial, level, zz)
        there = both(there, served(level, z, zz))
        return there, copy(st.at[slot, 2], qb.at[level, z], s_q.at[level, i], r_q.at[level, z], at_z(zz))

    def x_copy(level, zs):
        dst = kv.at[level, xh, zs]
        return copy(dst, dst, s_x.at[level, zs], r_x.at[level, zs], partner)

    def slot_of(level):
        if levels == 1:
            return here[0][1]
        first = 1 - jnp.minimum(level, 1)
        return first * z + (1 - first) * (4 + 4 * level + rem(z, 4))

    def source_of(level, i):
        if levels == 1:
            return rem(z + around(i, c), 8)
        first = 1 - jnp.minimum(level, 1)
        return rem(z + first * around(i, c) + (1 - first) * shared(rem(i, 4)), 8)

    def last_of(level):
        return 7 if levels == 1 else 7 - 4 * jnp.minimum(level, 1)

    def o_copy(level, i):
        zz = source_of(level, i)
        slot = slot_of(level)
        return copy(ost.at[level, zz], at.at[slot], s_o.at[level, i], r_o.at[slot], at_z(zz))

    here = [hosted(spatial, level, z) for level in range(levels)]

    def t_copy(d):
        ff = rem(f + d, 8)
        rows = pl.ds(pl.multiple_of(ff * PART, PART), PART)
        return copy(
            stt.at[:, :, rows],
            tb.at[:, :, pl.ds(pl.multiple_of(f * PART, PART), PART)],
            s_t.at[d], r_t.at[f], at_frame(ff),
        )

    def to_copy(d):
        ff = rem(f + d, 8)
        return copy(
            ot.at[:, pl.ds(pl.multiple_of(ff * PART, PART), PART)],
            at.at[pl.ds(spatial, temporal), pl.ds(pl.multiple_of(f * PART, PART), PART)],
            s_to.at[d], r_to.at[f], at_frame(ff),
        )

    for way in range(2):
        wz_copy(way, 0).start()
    wc_copy(z, own=True).start()

    def held_by(j):
        return sum((places[i] == j).astype(jnp.int32) * i for i in range(1, HEADS))

    def split(i, carry):
        cols = pl.ds(pl.multiple_of(i * HEAD, HEAD), HEAD)
        raw[i, 0] = k_in[0, :, cols]
        raw[i, 1] = v_in[0, :, cols]
        raw[i, 2] = q_in[0, :, cols]
        return carry

    def stage_spatial(j, carry):
        head = held_by(j)
        st[j, 0] = raw[head, 0]
        for a in range(0, ROWS, HEAD):
            st[j, 1, a : a + HEAD] = raw[head, 1, a : a + HEAD].T
        st[j, 2] = raw[head, 2]
        return carry

    def stage_temporal(t, carry):
        stt[t] = raw[held_by(first_t + t)]
        return carry

    lax.fori_loop(0, HEADS, split, 0)
    lax.fori_loop(0, spatial, stage_spatial, 0)

    def send_kv(i):
        for level in range(levels):
            there, one = kv_copy(level, i)
            only(there, one.start)

    def send_q(i, carry):
        for level in range(levels):
            there, one = q_copy(level, i)
            only(there, one.start)
        return carry

    def relay_kv(zs):
        for level in range(levels):
            def go(level=level):
                dst = kv.at[level, xh, zs]
                copy(dst, dst, s_kv.at[level, 0], r_kv.at[level, zs], twin).wait_recv()
                x_copy(level, zs).start()

            only(here[level][0], go)

    def pass_w(zs):
        wc_copy(zs).start()
        for way in range(2):
            wy_copy(zs * 2 + xh, way).start()
        wd_copy(zs * 2 + xh, 0).start()

    def at_step(i):
        return rem(z + around(i, c), 8)

    def near_step(i):
        return rem(z + near(i), 8)

    def keep_own():
        for level in range(levels):
            there, slot = here[level]

            def keep(level=level, slot=slot):
                kv[level, xh, z] = st[slot, pl.ds(0, 2)]
                qb[level, z] = st[slot, 2]
                x_copy(level, z).start()

            only(there, keep)
        wf[h, 0] = w_in[pl.ds(0, DEEP), :]
        wf[h, 1] = w_in[pl.ds(DEEP, DEEP), :]

    own_rows = pl.ds(pl.multiple_of(f * PART, PART), PART)

    def hop_w(hop):
        for way in range(2):
            wz_landed(way, hop)
            if hop < 3:
                wz_copy(way, hop + 1).start()

    ones_cols = jnp.ones((ROWS, HEAD), jnp.bfloat16)
    lines = lax.broadcasted_iota(jnp.int32, (ROWS, ROWS), 0)
    across = lax.broadcasted_iota(jnp.int32, (ROWS, ROWS), 1)
    same = rem(lines, PART) == rem(across, PART)

    def some_temporal(first, count):
        ts = [first + a for a in range(count)]
        scores = [jnp.where(same, dot_nt(tb[t, 2], tb[t, 0]), -jnp.inf) for t in ts]
        tops = [jnp.max(one, axis=1, keepdims=True) for one in scores]
        weights = [jnp.exp2((one - top) * SCALE).astype(jnp.bfloat16) for one, top in zip(scores, tops)]
        for t, one in zip(ts, weights):
            both = jnp.dot(
                one, jnp.concatenate([tb[t, 1], ones_cols], axis=1), preferred_element_type=jnp.float32
            )
            ot[t] = (both[:, :HEAD] / both[:, HEAD:]).astype(jnp.bfloat16)

    def attend_temporal():
        for d in range(1, 8):
            ff = rem(f + d, 8)
            dst = tb.at[:, :, pl.ds(pl.multiple_of(ff * PART, PART), PART)]
            copy(dst, dst, s_t.at[d], r_t.at[ff], twin).wait_recv()
        tb[:, :, own_rows] = stt[:, :, own_rows]
        lax.fori_loop(0, temporal // 3, lambda g, carry: some_temporal(3 * g, 3), None)
        if temporal % 3:
            some_temporal(temporal - temporal % 3, temporal % 3)
        for d in range(1, 8):
            to_copy(d).start()
        at[pl.ds(spatial, temporal), own_rows] = ot[:, own_rows]

    def w_step(i):
        zs = near_step(i)
        wc_landed(zs)
        for way in range(2):
            wy_copy(zs * 2 + 1 - xh, way).start()
        wd_copy(zs * 2 + 1 - xh, 0).start()

        @pl.when(i > 0)
        def _():
            wy_landed(zs * 2 + xh)
            wd_copy(zs * 2 + xh, 1).start()
            before = near_step(i - 1) * 2 + 1 - xh
            wy_landed(before)
            wd_copy(before, 1).start()

    doings = {
        "kv": send_kv,
        "t": lambda d: t_copy(d).start(),
        "q": lambda i: lax.fori_loop(0, 7, send_q, 0),
        "own": lambda i: keep_own(),
        "stage": lambda i: lax.fori_loop(0, temporal, stage_temporal, 0),
        "hop": hop_w,
        "pass": lambda i: pass_w(near_step(i)),
        "relay": lambda i: relay_kv(at_step(i)),
        "temporal": lambda i: attend_temporal(),
        "across": w_step,
    }
    early = 0
    for what, number in ORDER:
        doings[what](number)
        early += what == "across"

    def partner_kv(zs):
        for level in range(levels):
            def go(level=level):
                dst = kv.at[level, 1 - xh, zs]
                copy(dst, dst, s_x.at[level, 0], r_x.at[level, zs], partner).wait_recv()

            only(here[level][0], go)

    for zs in range(8):
        partner_kv(zs)

    block = 2 * ROWS
    blocks = HEADS * ROWS // block
    ones_rows = jnp.ones((16, block), jnp.bfloat16)
    lowest = jnp.full((32, ROWS), -jnp.inf, jnp.float32)

    def scores_of(level, zs, n, slot):
        keys = kv[level, n // 4, pl.ds(2 * (n % 4), 2), 0].reshape(block, HEAD)
        scores = dot_nt(keys, qb[level, zs])
        sbuf[slot * blocks + n] = scores
        return jnp.max(scores.reshape(block // 32, 32, ROWS), axis=0)

    def values_of(level, n):
        parts = [
            kv[level, n // 4, 2 * (n % 4) + a, 1, b : b + HEAD] for a in range(2) for b in range(0, ROWS, HEAD)
        ]
        return jnp.concatenate([jnp.concatenate(parts, axis=1), ones_rows], axis=0)

    def first_scores(level):
        def some(m, top):
            for a in range(4):
                top = jnp.maximum(top, scores_of(level, source_of(level, 0), 4 * m + a, 0))
            return top

        tops[0] = jnp.max(lax.fori_loop(0, blocks // 4, some, lowest), axis=0, keepdims=True)

    def attend(level, zs, later, slot):
        top, next_top = tops[slot], lowest
        for n in range(blocks):
            weights = jnp.exp2((sbuf[slot * blocks + n] - top) * SCALE).astype(jnp.bfloat16)
            part = jnp.dot(values_of(level, n), weights, preferred_element_type=jnp.float32)
            next_top = jnp.maximum(next_top, scores_of(level, later, n, 1 - slot))
            if n == 0:
                acc[...] = part
            else:
                acc[...] += part
        tops[1 - slot] = jnp.max(next_top, axis=0, keepdims=True)
        return (acc[:HEAD] / acc[HEAD : HEAD + 1]).T.astype(jnp.bfloat16)

    def spatial_chunk(level, slot_here, i):
        last = last_of(level)
        zs, later = source_of(level, i), source_of(level, rem(i + 1, 8))

        @pl.when(i == 0)
        def _():
            dst = qb.at[level, zs]
            copy(dst, dst, s_q.at[level, 0], r_q.at[level, zs], twin).wait_recv()
            first_scores(level)

        @pl.when(i + 1 < last)
        def _():
            dst = qb.at[level, later]
            copy(dst, dst, s_q.at[level, 0], r_q.at[level, later], twin).wait_recv()

        ost[level, zs] = attend(level, zs, later, rem(i, 2))

        @pl.when(i < last)
        def _():
            o_copy(level, i).start()

        @pl.when(i == last)
        def _():
            at[slot_here] = ost[level, zs]

    def step(n, carry):
        if levels == 1:
            only(here[0][0], functools.partial(spatial_chunk, 0, here[0][1], n))
        else:
            past = div(n, 8)
            level = past * (div(n, 4) - 1)
            i = n - past * 4 * (level + 1)
            there = (level == 0) | (rem(z, 4) < spatial - 4 - 4 * level)
            pl.when(there)(functools.partial(spatial_chunk, level, slot_of(level), i))
        pl.when(n < 8 - early)(lambda: w_step(n + early))
        return carry

    lax.fori_loop(0, 4 + 4 * levels, step, 0)
    last = near_step(7) * 2 + 1 - xh
    wy_landed(last)
    wd_copy(last, 1).start()

    for d in range(1, 8):
        ff = rem(f + d, 8)
        dst = at.at[pl.ds(spatial, temporal), pl.ds(pl.multiple_of(ff * PART, PART), PART)]
        copy(dst, dst, s_to.at[d], r_to.at[ff], twin).wait_recv()

    def o_landed(i, carry):
        zz = rem(z + around(i, c), 8)
        for level in range(levels):
            there, slot = hosted(spatial, level, zz)
            there = both(there, served(level, z, zz))

            def go(level=level, slot=slot):
                dst = at.at[slot]
                copy(dst, dst, s_o.at[level, 0], r_o.at[slot], twin).wait_recv()

            only(there, go)
        return carry

    lax.fori_loop(0, 7, o_landed, 0)
    for i in range(HEADS):
        where_at = places[i] + kinds[i] * (spatial - first_t)
        cat[:, i * HEAD : (i + 1) * HEAD] = at[where_at]

    def wd_wait(hh, carry):
        pl.when(hh != h)(lambda: wd_landed(hh))
        return carry

    lax.fori_loop(0, HEADS, wd_wait, 0)

    def project(n, carry):
        cols = pl.ds(pl.multiple_of(n * 512, 512), 512)
        out[0, :, cols] = jnp.dot(
            cat[...], wf[:, :, :, cols].reshape(HEADS * HEAD, 512), preferred_element_type=jnp.float32
        ).astype(jnp.bfloat16)
        return carry

    lax.fori_loop(0, WIDE // 512, project, 0)

    def sent(i, carry):
        zz = rem(z + around(i, c), 8)
        for level in range(levels):
            for one_copy in (kv_copy, q_copy):
                there, one = one_copy(level, i)
                only(there, one.wait_send)
            mine_here = here[level][0] if level == 0 else here[level][0] & (i < 3)
            only(mine_here, lambda level=level: o_copy(level, i).wait_send())
        wc_copy(zz).wait_send()
        for way in range(2):
            wy_copy(zz * 2 + xh, way).wait_send()
            wd_copy(zz * 2 + xh, way).wait_send()
        return carry

    lax.fori_loop(0, 7, sent, 0)
    wc_copy(z).wait_send()
    for way in range(2):
        for hop in range(4):
            wz_copy(way, hop).wait_send()

    def sent_more(zs, carry):
        for level in range(levels):
            only(here[level][0], lambda level=level: x_copy(level, zs).wait_send())
        for way in range(2):
            wy_copy(zs * 2 + 1 - xh, way).wait_send()
            wd_copy(zs * 2 + 1 - xh, way).wait_send()
        return carry

    lax.fori_loop(0, 8, sent_more, 0)
    for d in range(1, 8):
        t_copy(d).wait_send()
        to_copy(d).wait_send()


def layer(number, spatial, temporal, head_class, queries, keys, values, w_out):
    levels = levels_of(spatial)
    bf16, f32, dma = jnp.bfloat16, jnp.float32, pltpu.SemaphoreType.DMA
    whole = pl.BlockSpec(memory_space=pltpu.VMEM)
    return pl.pallas_call(
        functools.partial(kernel, spatial, temporal),
        out_shape=jax.ShapeDtypeStruct((1, ROWS, WIDE), bf16),
        in_specs=[pl.BlockSpec(memory_space=pltpu.SMEM)] + [whole] * 4,
        out_specs=whole,
        scratch_shapes=[
            pltpu.VMEM((HEADS, 3, ROWS, HEAD), bf16),
            pltpu.VMEM((spatial, 3, ROWS, HEAD), bf16),
            pltpu.VMEM((temporal, 3, ROWS, HEAD), bf16),
            pltpu.VMEM((levels, 2, 8, 2, ROWS, HEAD), bf16),
            pltpu.VMEM((levels, 8, ROWS, HEAD), bf16),
            pltpu.VMEM((temporal, 3, ROWS, HEAD), bf16),
            pltpu.VMEM((temporal, ROWS, HEAD), bf16),
            pltpu.VMEM((levels, 8, ROWS, HEAD), bf16),
            pltpu.VMEM((spatial + temporal, ROWS, HEAD), bf16),
            pltpu.VMEM((ROWS, HEADS * HEAD), bf16),
            pltpu.VMEM((HEADS, 2, DEEP, WIDE), bf16),
            pltpu.VMEM((HEADS, 2 * ROWS, ROWS), f32),
            pltpu.VMEM((HEAD + 16, ROWS), f32),
            pltpu.VMEM((2, 1, ROWS), f32),
        ]
        + [dma((levels, 8))] * 7 + [dma((HEADS,))]
        + [dma((8,))] * 4
        + [dma((2, 4))] * 2 + [dma((8,))] * 2 + [dma((2, HEADS))] * 4,
        compiler_params=pltpu.CompilerParams(
            collective_id=number, has_side_effects=True, vmem_limit_bytes=56 * 2**20
        ),
        name=f"layer_{spatial}",
    )(head_class, queries, keys, values, w_out)


def on_device(queries, keys, values, head_class, w_out):
    n_spatial = jnp.sum((head_class == 0).astype(jnp.int32))
    plans, below = [], 0
    for number, spatial in enumerate(PLANS):
        plans.append(functools.partial(layer, number, spatial, HEADS - below - 1))
        below = spatial
    which = sum((n_spatial > spatial).astype(jnp.int32) for spatial in PLANS[:-1])
    operands = (head_class, queries, keys, values, w_out)
    return lax.switch(which, plans, *operands)


def solution(mesh):
    placed = (
        P(("rep", "frame"), "head", None),
        P(("rep", "frame"), "head", None),
        P(("rep", "frame"), "head", None),
        P(),
        P("head", None),
    )
    return jax.shard_map(
        on_device,
        mesh=mesh,
        in_specs=placed,
        out_specs=P(("rep", "frame"), "head", None),
        check_vma=False,
    )
```
